512 devices in a mesh: res: 128 (over y, x, z_lo), depth: 4 (over z_hi, core).
Axes of the slice: x: 4, y: 4, z: 16 (z_hi: 2, z_lo: 8; z = z_hi * 8 + z_lo), core: 2. Of those that a mesh axis runs over, the one named last changes fastest.
Arguments:
- alignment_embedding: bfloat16 [512, 512, 256], P('depth', 'res'), may hold values from -6 to 6
- standardizer_gain: float32 [256], replicated, may hold values from 0.1 to 1.9
- standardizer_offset: float32 [256], replicated, may hold values from -3 to 3
- first_factor_matrix: bfloat16 [256, 32], replicated, may hold values from -0.375 to 0.375
- first_factor_offset: float32 [32], replicated, may hold values from -0.6 to 0.6
- second_factor_matrix: bfloat16 [256, 32], replicated, may hold values from -0.375 to 0.375
- second_factor_offset: float32 [32], replicated, may hold values from -0.6 to 0.6
- final_mapping_matrix: bfloat16 [1024, 128], replicated, may hold values from -4 to 4
- final_offset_entries: float32 [128], replicated, may hold values from -3 to 3
Outputs:
- pair: bfloat16 [512, 512, 128], P(('res', 'depth'))
The draws below stay inside these ranges and needn't reach their ends.
All inputs are finite; a program needn't handle non-finite values.
Results may differ from the reference program's by a relative error of at most 0.015.
Values may be sent and summed in bfloat16 or wider, within the bound.
No kernel may reach another device: no remote copies, remote signals or barrier semaphores. Data moves between devices by JAX's collectives and lax.ppermute only.
A program may use at most 64 MiB of HBM per device.

```python
import jax
import jax.numpy as jnp
from jax import lax

FEATURE_COUNT = 256
FACTOR_DEPTH = 32
CZ = 128
S_DEV = 128
AMINO_SITES = 512
ALIGNED_CHAINS = 512


def block_scale(stream_key, dims, shards, low, largest):
    gain = 1.0
    for axis_at, parts in shards:
        heights = jax.random.uniform(jax.random.fold_in(jax.random.fold_in(stream_key, 6), axis_at), (parts,), jnp.float32, low / len(shards), largest / len(shards))
        gain = gain * jnp.repeat(jnp.exp(heights), dims[axis_at] // parts).reshape((-1,) + (1,) * (len(dims) - 1 - axis_at))
    return gain


def scatter_about(rng, extent, width, most, cuts=(), dtype=jnp.bfloat16):
    drawn = jax.random.normal(rng, extent, jnp.float32) * width
    if len(cuts) > 0:
        drawn = block_scale(rng, extent, cuts, -0.22, 0.18) * drawn
    return jnp.clip(drawn, min=-most, max=most).astype(dtype)


def setup_inputs(seed: int = 0) -> dict:
    key_list = jax.random.split(jax.random.key(seed), 10)
    return {
        "alignment_embedding": scatter_about(key_list[0], (ALIGNED_CHAINS, AMINO_SITES, FEATURE_COUNT), 1.0, 6.0, ((0, 4), (1, 128))),
        "standardizer_gain": jnp.clip(1.0 + 0.18 * jax.random.normal(key_list[1], (FEATURE_COUNT,), jnp.float32), 0.1, 1.9),
        "standardizer_offset": scatter_about(key_list[2], (FEATURE_COUNT,), 0.5, 3.0, (), jnp.float32),
        "first_factor_matrix": scatter_about(key_list[3], (FEATURE_COUNT, FACTOR_DEPTH), FEATURE_COUNT ** -0.5, 0.375),
        "first_factor_offset": scatter_about(key_list[4], (FACTOR_DEPTH,), 0.1, 0.6, (), jnp.float32),
        "second_factor_matrix": scatter_about(key_list[5], (FEATURE_COUNT, FACTOR_DEPTH), FEATURE_COUNT ** -0.5, 0.375),
        "second_factor_offset": scatter_about(key_list[6], (FACTOR_DEPTH,), 0.1, 0.6, (), jnp.float32),
        "final_mapping_matrix": scatter_about(key_list[7], (FACTOR_DEPTH * FACTOR_DEPTH, CZ), (FACTOR_DEPTH * FACTOR_DEPTH // ALIGNED_CHAINS) ** -0.5, 4.0),
        "final_offset_entries": scatter_about(key_list[8], (CZ,), 0.5, 3.0, (), jnp.float32),
    }


def standardize_features(alignment_embedding, standardizer_gain, standardizer_offset):
    entry_tensor = alignment_embedding.astype(jnp.float32)
    centre = lax.optimization_barrier(jnp.mean(entry_tensor, axis=-1, keepdims=True))
    spread = lax.optimization_barrier(jnp.mean((entry_tensor - centre) ** 2, axis=-1, keepdims=True))
    return ((entry_tensor - centre) * lax.rsqrt(spread + 1e-05) * standardizer_gain + standardizer_offset).astype(jnp.bfloat16)

def reference(alignment_embedding, standardizer_gain, standardizer_offset, first_factor_matrix, first_factor_offset, second_factor_matrix, second_factor_offset, final_mapping_matrix, final_offset_entries):
    standardized_alignment = standardize_features(alignment_embedding, standardizer_gain, standardizer_offset).reshape(ALIGNED_CHAINS * AMINO_SITES, FEATURE_COUNT)
    left = (jnp.dot(standardized_alignment, first_factor_matrix, preferred_element_type=jnp.float32) + first_factor_offset).astype(jnp.bfloat16)
    right = (jnp.dot(standardized_alignment, second_factor_matrix, preferred_element_type=jnp.float32) + second_factor_offset).astype(jnp.bfloat16)
    groups = ALIGNED_CHAINS // S_DEV
    left_grp = left.reshape(groups, S_DEV, AMINO_SITES, FACTOR_DEPTH).astype(jnp.float32)
    right_grp = right.reshape(groups, S_DEV, AMINO_SITES, FACTOR_DEPTH).astype(jnp.float32)
    w_three = final_mapping_matrix.astype(jnp.float32).reshape(FACTOR_DEPTH, FACTOR_DEPTH, CZ)
    block = 4

    def rows(start):
        chosen = lax.dynamic_slice_in_dim(left_grp, start, block, 2)
        outer = jnp.einsum('gsic,gsje->gicje', chosen, right_grp) * (1.0 / ALIGNED_CHAINS)
        outer = outer.astype(jnp.bfloat16).astype(jnp.float32)
        return jnp.einsum('gicje,cez->ijz', outer, w_three)
    starts = (jnp.arange(AMINO_SITES // block) * block).astype(jnp.int32)
    summed = lax.map(rows, starts).reshape(AMINO_SITES, AMINO_SITES, CZ)
    return (summed + final_offset_entries).astype(jnp.bfloat16)
```

```python
import jax
import jax.numpy as jnp
from jax import lax
from jax.experimental import pallas as pl
from jax.experimental.pallas import tpu as pltpu
from jax.sharding import Mesh, PartitionSpec as P

F32 = jnp.float32
BF16 = jnp.bfloat16
AXES = ("y", "x", "zq", "zp", "zh", "core")
SWAP = [(0, 1), (1, 0)]
NT = (((1,), (1,)), ((), ()))


def project(x_ref, gain_ref, offset_ref, matrix_ref, bias_ref):
    x = x_ref[...].astype(F32)
    centre = jnp.mean(x, axis=-1, keepdims=True)
    shifted = x - centre
    spread = jnp.mean(shifted * shifted, axis=-1, keepdims=True)
    normed = shifted * lax.rsqrt(spread + 1e-05) * gain_ref[...].reshape(1, 1, -1)
    normed = normed + offset_ref[...].reshape(1, 1, -1)
    chain_rows, residue_rows, _ = x.shape
    chans = matrix_ref.shape[1]
    matrix = matrix_ref[...].astype(F32).T.astype(BF16)
    bias = jnp.broadcast_to(bias_ref[...], (chain_rows, chans)).T
    return [
        lax.dot_general(matrix, normed[:, r, :].astype(BF16), NT, preferred_element_type=F32) + bias
        for r in range(residue_rows)
    ]


def right_kernel(x_ref, gain_ref, offset_ref, matrix_ref, bias_ref, out_ref):
    parts = project(x_ref, gain_ref, offset_ref, matrix_ref, bias_ref)
    out_ref[...] = jnp.concatenate(parts, axis=0).astype(BF16)


def left_kernel(x_ref, gain_ref, offset_ref, matrix_ref, bias_ref, own_ref, other_ref):
    parts = project(x_ref, gain_ref, offset_ref, matrix_ref, bias_ref)
    first = jnp.concatenate(parts[:2], axis=0)
    second = jnp.concatenate(parts[2:], axis=0)
    low = lax.axis_index("zh") == 0
    own_ref[...] = jnp.where(low, first, second).astype(BF16)
    other_ref[...] = jnp.where(low, second, first).astype(BF16)


def pair_kernel(own_ref, near_ref, left_ref, map_ref, out_ref, a32, a16, x16, wide, res):
    zh = lax.axis_index("zh")
    zp = lax.axis_index("zp")
    for yx in range(16):
        for block in range(2):
            for ii in range(2):
                a32[pl.ds(block * 1024 + yx * 2 + ii, 32, stride=32), :] = left_ref[
                    yx, block, ii * 32 : ii * 32 + 32, :
                ].astype(F32)
    for block in range(2):
        a16[:, block * 128 : block * 128 + 128] = a32[block * 1024 : block * 1024 + 1024, :].astype(BF16)
    wide[...] = jnp.zeros_like(wide)
    for c in range(32):
        for r in range(4):
            wide[c * 128 + r * 32 : c * 128 + r * 32 + 32, r * 128 : r * 128 + 128] = map_ref[
                c * 32 : c * 32 + 32, :
            ]
    for zl in range(8):
        zq, parity = zl // 2, zl % 2
        mine = zp == parity
        blocks = []
        for src in (zh, 1 - zh):
            blocks.append(jnp.where(mine, own_ref[src * 4 + zq], near_ref[src * 4 + zq]))
        right = jnp.concatenate(blocks, axis=1)
        outer = lax.dot_general(a16[...], right, NT, preferred_element_type=F32).astype(BF16)
        for c in range(32):
            x16[zl * 32 : zl * 32 + 32, c * 128 : c * 128 + 128] = outer[c * 32 : c * 32 + 32, :]
    total = jnp.dot(x16[...], wide[...], preferred_element_type=F32) * (1.0 / 512)
    for r in range(4):
        res[r * 256 : r * 256 + 256, :] = total[:, r * 128 : r * 128 + 128]
    for r in range(4):
        for i in range(0, 32, 2):
            rows = [res[pl.ds(r * 256 + i + k, 8, stride=32), :] for k in range(2)]
            out_ref[i * 8 : i * 8 + 16, r * 128 : r * 128 + 128] = jnp.concatenate(rows, axis=0).astype(BF16)


def final_kernel(parts_ref, bias_ref, out_ref, rows):
    parts = parts_ref[...].astype(F32).reshape(16, 2, 8, 512)
    summed = (parts[:, 0] + parts[:, 1]).reshape(128, 512)
    for r in range(4):
        rows[pl.ds(r, 128, stride=4), :] = summed[:, r * 128 : r * 128 + 128] + bias_ref[...]
    out_ref[...] = rows[...].astype(BF16)


def params(mib):
    return pltpu.CompilerParams(vmem_limit_bytes=mib * 2**20)


def local(x, gain, offset, first, first_bias, second, second_bias, mapping, final_bias):
    gain, offset = gain.reshape(1, -1), offset.reshape(1, -1)
    right = pl.pallas_call(
        right_kernel,
        out_shape=jax.ShapeDtypeStruct((128, 128), BF16),
        compiler_params=params(16),
        name="right_projection",
    )(x, gain, offset, second, second_bias.reshape(1, -1))
    half = jax.ShapeDtypeStruct((64, 128), BF16)
    left_own, left_other = pl.pallas_call(
        left_kernel,
        out_shape=(half, half),
        compiler_params=params(16),
        name="left_projection",
    )(x, gain, offset, first, first_bias.reshape(1, -1))

    own = lax.all_to_all(jnp.broadcast_to(right[None], (8, 128, 128)), ("zh", "zq"), 0, 0)
    left_got = lax.ppermute(left_other, "zh", SWAP)
    left = jnp.stack([left_own, left_got])
    left, own = lax.optimization_barrier((left, own))
    near = lax.ppermute(own, "zp", SWAP)
    left = lax.all_to_all(jnp.broadcast_to(left[None], (16, 2, 64, 128)), ("y", "x"), 0, 0)

    parts = pl.pallas_call(
        pair_kernel,
        out_shape=jax.ShapeDtypeStruct((256, 512), BF16),
        scratch_shapes=[
            pltpu.VMEM((2048, 128), F32),
            pltpu.VMEM((1024, 256), BF16),
            pltpu.VMEM((256, 4096), BF16),
            pltpu.VMEM((4096, 512), BF16),
            pltpu.VMEM((1024, 128), F32),
        ],
        compiler_params=params(40),
        name="pair_block",
    )(own, near, left, mapping)
    parts = lax.all_to_all(parts.reshape(32, 8, 512), ("y", "x", "core"), 0, 0)
    out = pl.pallas_call(
        final_kernel,
        out_shape=jax.ShapeDtypeStruct((512, 128), BF16),
        scratch_shapes=[pltpu.VMEM((512, 128), F32)],
        compiler_params=params(16),
        name="sum_and_bias",
    )(parts.reshape(256, 512), final_bias.reshape(1, -1))
    return out.reshape(1, 512, 128)


def solution(mesh):
    fine = Mesh(mesh.devices.reshape(4, 4, 4, 2, 2, 2), AXES)
    placed = (P(("zh", "core"), ("y", "x", "zq", "zp"), None),) + (P(),) * 8
    return jax.shard_map(
        local, mesh=fine, in_specs=placed, out_specs=P(AXES, None, None), check_vma=False
    )
```

```python
import jax
import jax.numpy as jnp
from jax import lax
from jax.experimental import pallas as pl
from jax.experimental.pallas import tpu as pltpu
from jax.sharding import Mesh, PartitionSpec as P

F32 = jnp.float32
BF16 = jnp.bfloat16
AXES = ("y", "x", "zu", "zv", "zp", "zh", "core")
RING = ("zu", "zv", "zp", "zh")
NT = (((1,), (1,)), ((), ()))


def projection_kernel(x_hbm, gain_hbm, offset_hbm, left_hbm, left_bias_hbm, right_hbm, right_bias_hbm, right_out, left_out, far_ref, x_ref, gain_ref, offset_ref, left_ref, left_bias_ref, right_ref, right_bias_ref, sems):
    pairs = (
        (x_hbm, x_ref),
        (gain_hbm, gain_ref),
        (offset_hbm, offset_ref),
        (left_hbm, left_ref),
        (left_bias_hbm, left_bias_ref),
        (right_hbm, right_ref),
        (right_bias_hbm, right_bias_ref),
    )
    copies = [pltpu.make_async_copy(src, dst, sems.at[k]) for k, (src, dst) in enumerate(pairs)]
    for copy in copies:
        copy.start()
    for copy in copies:
        copy.wait()
    x = x_ref[...].astype(F32)
    centre = jnp.mean(x, axis=-1, keepdims=True)
    shifted = x - centre
    spread = jnp.mean(shifted * shifted, axis=-1, keepdims=True)
    normed = shifted * lax.rsqrt(spread + 1e-05) * gain_ref[...].reshape(1, 1, 256)
    normed = normed + offset_ref[...].reshape(1, 1, 256)
    both = jnp.concatenate([right_ref[...], left_ref[...]], axis=0)
    bias = jnp.concatenate([right_bias_ref[...], left_bias_ref[...]], axis=1)
    bias = jnp.broadcast_to(bias, (128, 64)).T
    rows = [
        (
            lax.dot_general(both, normed[:, r, :].astype(BF16), NT, preferred_element_type=F32)
            + bias
        ).astype(BF16)
        for r in range(4)
    ]
    right_out[...] = jnp.concatenate([row[:32] for row in rows], axis=0)
    far_ref[:128, :] = right_out[...]
    first = jnp.concatenate([rows[0][32:], rows[1][32:]], axis=0)
    second = jnp.concatenate([rows[2][32:], rows[3][32:]], axis=0)
    low = lax.axis_index("zh") == 0
    left_out[...] = jnp.where(low, first, second)
    far_ref[128:, :] = jnp.where(low, second, first)


def arrange_kernel(left_ref, right_ref, far_ref, below_ref, above_ref, left_out, right_out):
    half, upper = lax.axis_index("zh"), lax.axis_index("zu")
    own, far = left_ref[...], far_ref[128:, :]
    first, second = jnp.where(half == 0, own, far), jnp.where(half == 0, far, own)
    for to in range(16):
        left_out[to, 0] = first
        left_out[to, 1] = second
    here = half * 2 + upper
    right_out[here] = right_ref[...]
    right_out[(here + 2) % 4] = far_ref[:128, :]
    right_out[(here + 3) % 4] = below_ref[...]
    right_out[(here + 1) % 4] = above_ref[...]


def pair_kernel(near0, near1, near2, near3, left_ref, map_ref, bias_ref, out_ref, bias_out, a32, a16, x16, wide_ref, res):
    place = lax.axis_index("zv") * 2 + lax.axis_index("zp")
    for yx in range(16):
        for block in range(2):
            for ii in range(2):
                a32[pl.ds(block * 1024 + yx * 2 + ii, 32, stride=32), :] = left_ref[
                    yx, block, ii * 32 : ii * 32 + 32, :
                ].astype(F32)
    for block in range(2):
        a16[:, block * 128 : block * 128 + 128] = a32[block * 1024 : block * 1024 + 1024, :].astype(BF16)
    bias_out[...] = bias_ref[...]
    wide_ref[...] = jnp.zeros_like(wide_ref)
    for c in range(32):
        for r in range(4):
            wide_ref[c * 128 + r * 32 : c * 128 + r * 32 + 32, r * 128 : r * 128 + 128] = map_ref[
                c * 32 : c * 32 + 32, :
            ]
    for k, near in ((0, near0), (-1, near1), (1, near2), (2, near3)):
        for zu in range(2):
            zl = zu * 4 + (place + k + 4) % 4
            row = pl.multiple_of(zl * 32, 32)
            right = jnp.concatenate([near[zu], near[2 + zu]], axis=1)
            outer = lax.dot_general(a16[...], right, NT, preferred_element_type=F32).astype(BF16)
            for c in range(32):
                x16[pl.ds(row, 32), c * 128 : c * 128 + 128] = outer[c * 32 : c * 32 + 32, :]
    total = jnp.dot(x16[...], wide_ref[...], preferred_element_type=F32) * (1.0 / 512)
    for r in range(4):
        res[r * 256 : r * 256 + 256, :] = total[:, r * 128 : r * 128 + 128]
    for r in range(4):
        for i in range(0, 32, 2):
            rows = [res[pl.ds(r * 256 + i + k, 8, stride=32), :] for k in range(2)]
            out_ref[i * 8 : i * 8 + 16, r * 128 : r * 128 + 128] = jnp.concatenate(rows, axis=0).astype(BF16)


def final_kernel(parts_ref, bias_ref, out_ref, rows):
    parts = parts_ref[...].astype(F32).reshape(16, 2, 8, 512)
    summed = (parts[:, 0] + parts[:, 1]).reshape(128, 512)
    for r in range(4):
        rows[pl.ds(r, 128, stride=4), :] = summed[:, r * 128 : r * 128 + 128] + bias_ref[...]
    out_ref[...] = rows[...].astype(BF16)


def params(mib):
    return pltpu.CompilerParams(vmem_limit_bytes=mib * 2**20)


def shape(*dims, dtype=BF16):
    return jax.ShapeDtypeStruct(dims, dtype)


def from_ring(value, step):
    place = [z % 8 * 2 + z // 8 for z in range(16)]
    return lax.ppermute(value, RING, [(place[(z + step) % 16], place[z]) for z in range(16)])


def local(x, gain, offset, first, first_bias, second, second_bias, mapping, final_bias):
    operands = (
        x,
        gain.reshape(1, 256),
        offset.reshape(1, 256),
        first.T,
        first_bias.reshape(1, 32),
        second.T,
        second_bias.reshape(1, 32),
    )
    right, left, far = pl.pallas_call(
        projection_kernel,
        out_shape=(shape(128, 128), shape(64, 128), shape(192, 128)),
        in_specs=[pl.BlockSpec(memory_space=pltpu.HBM)] * 7,
        scratch_shapes=[pltpu.VMEM(a.shape, a.dtype) for a in operands] + [pltpu.SemaphoreType.DMA((7,))],
        compiler_params=params(60),
        name="projections",
    )(*operands)
    far = from_ring(far, 8)
    below, above = from_ring(right, -4), from_ring(right, 4)
    left, right = pl.pallas_call(
        arrange_kernel,
        out_shape=(shape(16, 2, 64, 128), shape(4, 128, 128)),
        compiler_params=params(16),
        name="arrange",
    )(left, right, far, below, above)
    left = lax.all_to_all(left, ("y", "x"), 0, 0)
    near = [from_ring(right, step) for step in (-1, 1, 2)]

    parts, bias = pl.pallas_call(
        pair_kernel,
        out_shape=(shape(256, 512), shape(1, 128, dtype=F32)),
        scratch_shapes=[
            pltpu.VMEM((2048, 128), F32),
            pltpu.VMEM((1024, 256), BF16),
            pltpu.VMEM((256, 4096), BF16),
            pltpu.VMEM((4096, 512), BF16),
            pltpu.VMEM((1024, 128), F32),
        ],
        compiler_params=params(20),
        name="pair_block",
    )(right, *near, left, mapping, final_bias.reshape(1, 128))
    parts = lax.all_to_all(parts.reshape(32, 8, 512), ("y", "x", "core"), 0, 0)
    out = pl.pallas_call(
        final_kernel,
        out_shape=shape(512, 128),
        scratch_shapes=[pltpu.VMEM((512, 128), F32)],
        compiler_params=params(16),
        name="sum_and_bias",
    )(parts.reshape(256, 512), bias)
    return out.reshape(1, 512, 128)


def solution(mesh):
    fine = Mesh(mesh.devices.reshape(4, 4, 2, 2, 2, 2, 2), AXES)
    placed = (P(("zh", "core"), ("y", "x", "zu", "zv", "zp"), None),) + (P(),) * 8
    return jax.shard_map(
        local, mesh=fine, in_specs=placed, out_specs=P(AXES, None, None), check_vma=False
    )
```

```python
import jax
import jax.numpy as jnp
from jax import lax
from jax.experimental import pallas as pl
from jax.experimental.pallas import tpu as pltpu
from jax.sharding import Mesh, PartitionSpec as P

F32 = jnp.float32
BF16 = jnp.bfloat16
AXES = ("y", "x", "zu", "zv", "zp", "zh", "core")
SWAP = [(0, 1), (1, 0)]
NT = (((1,), (1,)), ((), ()))


def projection_kernel(
    x_hbm, gain_hbm, offset_hbm, left_hbm, left_bias_hbm, right_hbm, right_bias_hbm, map_hbm, bias_hbm,
    out_ref, map_out,
    x_ref, gain_ref, offset_ref, left_ref, left_bias_ref, right_ref, right_bias_ref, map_ref, bias_ref, sems,
):
    sources = (x_hbm, gain_hbm, offset_hbm, left_hbm, left_bias_hbm, right_hbm, right_bias_hbm, map_hbm, bias_hbm)
    targets = (x_ref, gain_ref, offset_ref, left_ref, left_bias_ref, right_ref, right_bias_ref, map_ref, bias_ref)
    copies = [
        pltpu.make_async_copy(src, dst, sems.at[k]) for k, (src, dst) in enumerate(zip(sources, targets))
    ]
    for copy in copies:
        copy.start()
    for copy in copies[:7]:
        copy.wait()
    x = x_ref[...].astype(F32)
    centre = jnp.mean(x, axis=-1, keepdims=True)
    shifted = x - centre
    spread = jnp.mean(shifted * shifted, axis=-1, keepdims=True)
    normed = shifted * lax.rsqrt(spread + 1e-05) * gain_ref[...].reshape(1, 1, 256)
    normed = normed + offset_ref[...].reshape(1, 1, 256)
    both = jnp.concatenate([right_ref[...], left_ref[...]], axis=0)
    bias = jnp.concatenate([right_bias_ref[...], left_bias_ref[...]], axis=1)
    bias = jnp.broadcast_to(bias, (128, 64)).T
    for r in range(4):
        rows = lax.dot_general(both, normed[:, r, :].astype(BF16), NT, preferred_element_type=F32)
        rows = (rows + bias).astype(BF16)
        out_ref[r * 32 : r * 32 + 32, :] = rows[:32]
        out_ref[128 + r * 32 : 160 + r * 32, :] = rows[32:]
    for copy in copies[7:]:
        copy.wait()
    map_out[:1024, :] = map_ref[...].astype(F32)
    map_out[1024:, :] = jnp.broadcast_to(bias_ref[...], (8, 128))


def split_kernel(got_ref, right_out, left_out):
    first = lax.axis_index("core") == 0
    for block in range(2):
        right = got_ref[block, :128, :]
        for to in range(16):
            right_out[to, block] = right
        for half in range(2):
            row = 128 + half * 64
            left_out[block, half * 32 : half * 32 + 32, :] = jnp.where(
                first, got_ref[block, row : row + 32, :], got_ref[block, row + 32 : row + 64, :]
            )


def pair_kernel(left_ref, right_ref, map_ref, out_ref, bias_out, a32, a16, x16, wide_ref, res):
    bias_out[...] = map_ref[1024:1025, :]
    for t in range(8):
        zl = t % 2 * 4 + t // 2 % 2 * 2 + t // 4
        for block in range(2):
            for half in range(2):
                a32[pl.ds(block * 512 + zl * 2 + half, 32, stride=16), :] = left_ref[
                    t, block, half * 32 : half * 32 + 32, :
                ].astype(F32)
    for block in range(2):
        a16[:, block * 128 : block * 128 + 128] = a32[block * 512 : block * 512 + 512, :].astype(BF16)
    wide_ref[...] = jnp.zeros_like(wide_ref)
    for c in range(32):
        for r in range(4):
            wide_ref[c * 128 + r * 32 : c * 128 + r * 32 + 32, r * 128 : r * 128 + 128] = map_ref[
                c * 32 : c * 32 + 32, :
            ].astype(BF16)
    for yx in range(16):
        right = jnp.concatenate([right_ref[yx, 0], right_ref[yx, 1]], axis=1)
        outer = lax.dot_general(a16[...], right, NT, preferred_element_type=F32).astype(BF16)
        for c in range(32):
            x16[yx * 16 : yx * 16 + 16, c * 128 : c * 128 + 128] = outer[c * 16 : c * 16 + 16, :]
    total = jnp.dot(x16[...], wide_ref[...], preferred_element_type=F32) * (1.0 / 512)
    for r in range(4):
        res[r * 256 : r * 256 + 256, :] = total[:, r * 128 : r * 128 + 128]
    for k in range(8):
        for half in range(2):
            to = half * 8 + k
            for r in range(4):
                rows = res[pl.ds(r * 256 + k * 2 + half, 16, stride=16), :]
                out_ref[to, :, r * 128 : r * 128 + 128] = rows.astype(BF16)


def final_kernel(parts_ref, bias_ref, out_ref, rows):
    for zl in range(8):
        summed = parts_ref[zl].astype(F32) + parts_ref[8 + zl].astype(F32)
        for r in range(4):
            rows[pl.ds(zl * 4 + r, 16, stride=32), :] = summed[:, r * 128 : r * 128 + 128] + bias_ref[...]
    out_ref[...] = rows[...].astype(BF16)


def params(mib):
    return pltpu.CompilerParams(vmem_limit_bytes=mib * 2**20)


def shape(*dims, dtype=BF16):
    return jax.ShapeDtypeStruct(dims, dtype)


def local(x, gain, offset, first, first_bias, second, second_bias, mapping, final_bias):
    operands = (
        x,
        gain.reshape(1, 256),
        offset.reshape(1, 256),
        first.T,
        first_bias.reshape(1, 32),
        second.T,
        second_bias.reshape(1, 32),
    )
    operands += (mapping, final_bias.reshape(1, 128))
    both, mapping = pl.pallas_call(
        projection_kernel,
        out_shape=(shape(256, 128), shape(1032, 128, dtype=F32)),
        in_specs=[pl.BlockSpec(memory_space=pltpu.HBM)] * 9,
        scratch_shapes=[pltpu.VMEM(a.shape, a.dtype) for a in operands] + [pltpu.SemaphoreType.DMA((9,))],
        compiler_params=params(60),
        name="projections",
    )(*operands)
    both = lax.all_gather(both, "core", axis=0)
    right, left0 = pl.pallas_call(
        split_kernel,
        out_shape=(shape(16, 2, 128, 128), shape(2, 64, 128)),
        compiler_params=params(16),
        name="split",
    )(both)
    right = lax.all_to_all(right, ("y", "x"), 0, 0)
    left = left0
    for axis in ("zu", "zv", "zp"):
        left = lax.all_gather(left, axis, axis=0)
    left = left.reshape(8, 2, 64, 128)

    parts, bias = pl.pallas_call(
        pair_kernel,
        out_shape=(shape(16, 16, 512), shape(1, 128, dtype=F32)),
        scratch_shapes=[
            pltpu.VMEM((1024, 128), F32),
            pltpu.VMEM((512, 256), BF16),
            pltpu.VMEM((256, 4096), BF16),
            pltpu.VMEM((4096, 512), BF16),
            pltpu.VMEM((1024, 128), F32),
        ],
        compiler_params=params(20),
        name="pair_block",
    )(left, right, mapping)
    parts = lax.all_to_all(parts, ("zh", "zu", "zv", "zp"), 0, 0)
    out = pl.pallas_call(
        final_kernel,
        out_shape=shape(512, 128),
        scratch_shapes=[pltpu.VMEM((512, 128), F32)],
        compiler_params=params(16),
        name="sum_and_bias",
    )(parts, bias)
    return out.reshape(1, 512, 128)


def solution(mesh):
    fine = Mesh(mesh.devices.reshape(4, 4, 2, 2, 2, 2, 2), AXES)
    placed = (P(("zh", "core"), ("y", "x", "zu", "zv", "zp"), None),) + (P(),) * 8
    return jax.shard_map(
        local, mesh=fine, in_specs=placed, out_specs=P(AXES, None, None), check_vma=False
    )
```

```python
import jax
import jax.numpy as jnp
from jax import lax
from jax.experimental import pallas as pl
from jax.experimental.pallas import tpu as pltpu
from jax.sharding import Mesh, PartitionSpec as P

F32 = jnp.float32
BF16 = jnp.bfloat16
AXES = ("y", "x", "zu", "zv", "zp", "zh", "core")
SWAP = [(0, 1), (1, 0)]
NT = (((1,), (1,)), ((), ()))


def projection_kernel(
    x_hbm, gain_hbm, offset_hbm, left_hbm, left_bias_hbm, right_hbm, right_bias_hbm, map_hbm, bias_hbm,
    right_out, left_out, map_out,
    x_ref, gain_ref, offset_ref, left_ref, left_bias_ref, right_ref, right_bias_ref, map_ref, bias_ref, sems,
):
    sources = (x_hbm, gain_hbm, offset_hbm, left_hbm, left_bias_hbm, right_hbm, right_bias_hbm, map_hbm, bias_hbm)
    targets = (x_ref, gain_ref, offset_ref, left_ref, left_bias_ref, right_ref, right_bias_ref, map_ref, bias_ref)
    copies = [
        pltpu.make_async_copy(src, dst, sems.at[k]) for k, (src, dst) in enumerate(zip(sources, targets))
    ]
    for copy in copies:
        copy.start()
    source = lax.broadcasted_iota(jnp.int32, (512, 512), 0)
    target = lax.broadcasted_iota(jnp.int32, (512, 512), 1)
    move = (source == target % 128 * 4 + target // 128).astype(F32).astype(BF16)
    for copy in copies[1:7]:
        copy.wait()
    both = jnp.concatenate([right_ref[...], left_ref[...]], axis=0)
    bias = jnp.concatenate([right_bias_ref[...], left_bias_ref[...]], axis=1)
    bias = jnp.broadcast_to(bias, (128, 64)).T
    copies[0].wait()
    x = x_ref[...].astype(F32).reshape(512, 256)
    centre = jnp.mean(x, axis=-1, keepdims=True)
    shifted = x - centre
    spread = jnp.mean(shifted * shifted, axis=-1, keepdims=True)
    normed = shifted * lax.rsqrt(spread + 1e-05) * gain_ref[...] + offset_ref[...]
    rows = lax.dot_general(both, normed.astype(BF16), NT, preferred_element_type=F32)
    rows = (rows + jnp.concatenate([bias] * 4, axis=1)).astype(BF16)
    rows = jnp.dot(rows, move, preferred_element_type=F32).astype(BF16)
    for r in range(4):
        for to in range(16):
            right_out[to, r * 32 : r * 32 + 32, :] = rows[:32, r * 128 : r * 128 + 128]
        left_out[r * 32 : r * 32 + 32, :] = rows[32:, r * 128 : r * 128 + 128]
    for copy in copies[7:]:
        copy.wait()
    map_out[:1024, :] = map_ref[...].astype(F32)
    map_out[1024:, :] = jnp.broadcast_to(bias_ref[...], (8, 128))


def join_kernel(own_ref, other_ref, out_ref):
    here = lax.axis_index("zu")
    out_ref[here] = own_ref[...]
    out_ref[1 - here] = other_ref[...]


def pair_kernel(left_ref, right_ref, other_ref, map_ref, out_ref, bias_out, a32, a16, x16, wide_ref, res):
    bias_out[...] = map_ref[1024:1025, :]
    core = lax.axis_index("core")
    for block, source in enumerate((core, 1 - core)):
        for t in range(8):
            zl = t % 2 * 4 + t // 2 % 2 * 2 + t // 4
            for half in range(2):
                row = pl.multiple_of((half * 2 + core) * 32, 32)
                a32[pl.ds(block * 512 + zl * 2 + half, 32, stride=16), :] = left_ref[
                    source, t, pl.ds(row, 32), :
                ].astype(F32)
        a16[:, block * 128 : block * 128 + 128] = a32[block * 512 : block * 512 + 512, :].astype(BF16)
    wide_ref[...] = jnp.zeros_like(wide_ref)
    for c in range(32):
        for r in range(4):
            wide_ref[c * 128 + r * 32 : c * 128 + r * 32 + 32, r * 128 : r * 128 + 128] = map_ref[
                c * 32 : c * 32 + 32, :
            ].astype(BF16)
    for first in range(0, 16, 4):
        chips = range(first, first + 4)
        right = [jnp.concatenate([right_ref[yx], other_ref[yx]], axis=1) for yx in chips]
        right = jnp.concatenate(right, axis=0)
        outer = lax.dot_general(a16[...], right, NT, preferred_element_type=F32).astype(BF16)
        for k, yx in enumerate(chips):
            for c in range(32):
                x16[yx * 16 : yx * 16 + 16, c * 128 : c * 128 + 128] = outer[
                    c * 16 : c * 16 + 16, k * 128 : k * 128 + 128
                ]
    total = jnp.dot(x16[...], wide_ref[...], preferred_element_type=F32) * (1.0 / 512)
    for r in range(4):
        res[r * 256 : r * 256 + 256, :] = total[:, r * 128 : r * 128 + 128]
    for k in range(8):
        for half in range(2):
            to = half * 8 + k
            for r in range(4):
                rows = res[pl.ds(r * 256 + k * 2 + half, 16, stride=16), :]
                out_ref[to, :, r * 128 : r * 128 + 128] = rows.astype(BF16)


def final_kernel(parts_ref, bias_ref, out_ref, rows):
    for zl in range(8):
        summed = parts_ref[zl].astype(F32) + parts_ref[8 + zl].astype(F32)
        for r in range(4):
            rows[pl.ds(zl * 4 + r, 16, stride=32), :] = summed[:, r * 128 : r * 128 + 128] + bias_ref[...]
    out_ref[...] = rows[...].astype(BF16)


def params(mib):
    return pltpu.CompilerParams(vmem_limit_bytes=mib * 2**20)


def shape(*dims, dtype=BF16):
    return jax.ShapeDtypeStruct(dims, dtype)


def local(x, gain, offset, first, first_bias, second, second_bias, mapping, final_bias):
    operands = (
        x,
        gain.reshape(1, 256),
        offset.reshape(1, 256),
        first.T,
        first_bias.reshape(1, 32),
        second.T,
        second_bias.reshape(1, 32),
    )
    operands += (mapping, final_bias.reshape(1, 128))
    right, left, mapping = pl.pallas_call(
        projection_kernel,
        out_shape=(shape(16, 128, 128), shape(128, 128), shape(1032, 128, dtype=F32)),
        in_specs=[pl.BlockSpec(memory_space=pltpu.HBM)] * 9,
        scratch_shapes=[pltpu.VMEM(a.shape, a.dtype) for a in operands] + [pltpu.SemaphoreType.DMA((9,))],
        compiler_params=params(60),
        name="projections",
    )(*operands)
    right = lax.all_to_all(right, ("y", "x"), 0, 0)
    other = lax.ppermute(left, "zu", SWAP)
    left = pl.pallas_call(
        join_kernel,
        out_shape=shape(2, 128, 128),
        compiler_params=params(16),
        cost_estimate=pl.CostEstimate(flops=10**10, bytes_accessed=0, transcendentals=0),
        name="join",
    )(left, other)
    for axis in ("zv", "zp"):
        left = lax.all_gather(left, axis, axis=0)
    left, right = lax.optimization_barrier((left, right))
    right_other = lax.ppermute(right, "core", SWAP)
    left = lax.all_gather(left, "core", axis=0).reshape(2, 8, 128, 128)

    parts, bias = pl.pallas_call(
        pair_kernel,
        out_shape=(shape(16, 16, 512), shape(1, 128, dtype=F32)),
        scratch_shapes=[
            pltpu.VMEM((1024, 128), F32),
            pltpu.VMEM((512, 256), BF16),
            pltpu.VMEM((256, 4096), BF16),
            pltpu.VMEM((4096, 512), BF16),
            pltpu.VMEM((1024, 128), F32),
        ],
        compiler_params=params(20),
        name="pair_block",
    )(left, right, right_other, mapping)
    parts = lax.all_to_all(parts, ("zh", "zu", "zv", "zp"), 0, 0)
    out = pl.pallas_call(
        final_kernel,
        out_shape=shape(512, 128),
        scratch_shapes=[pltpu.VMEM((512, 128), F32)],
        compiler_params=params(16),
        name="sum_and_bias",
    )(parts, bias)
    return out.reshape(1, 512, 128)


def solution(mesh):
    fine = Mesh(mesh.devices.reshape(4, 4, 2, 2, 2, 2, 2), AXES)
    placed = (P(("zh", "core"), ("y", "x", "zu", "zv", "zp"), None),) + (P(),) * 8
    return jax.shard_map(
        local, mesh=fine, in_specs=placed, out_specs=P(AXES, None, None), check_vma=False
    )
```

```python
import jax
import jax.numpy as jnp
from jax import lax
from jax.experimental import pallas as pl
from jax.experimental.pallas import tpu as pltpu
from jax.sharding import Mesh, PartitionSpec as P

F32 = jnp.float32
BF16 = jnp.bfloat16
AXES = ("y", "x", "zu", "zv", "zp", "zh", "core")
SWAP = [(0, 1), (1, 0)]
NT = (((1,), (1,)), ((), ()))


def projection_kernel(
    x_hbm, gain_hbm, offset_hbm, left_hbm, left_bias_hbm, right_hbm, right_bias_hbm, map_hbm, bias_hbm,
    right_out, left_out, map_out,
    x_ref, gain_ref, offset_ref, left_ref, left_bias_ref, right_ref, right_bias_ref, map_ref, bias_ref, sems,
):
    sources = (x_hbm, gain_hbm, offset_hbm, left_hbm, left_bias_hbm, right_hbm, right_bias_hbm, map_hbm, bias_hbm)
    targets = (x_ref, gain_ref, offset_ref, left_ref, left_bias_ref, right_ref, right_bias_ref, map_ref, bias_ref)
    copies = [
        pltpu.make_async_copy(src, dst, sems.at[k]) for k, (src, dst) in enumerate(zip(sources, targets))
    ]
    for copy in copies:
        copy.start()
    source = lax.broadcasted_iota(jnp.int32, (512, 512), 0)
    target = lax.broadcasted_iota(jnp.int32, (512, 512), 1)
    move = (source == target % 128 * 4 + target // 128).astype(F32).astype(BF16)
    for copy in copies[1:7]:
        copy.wait()
    both = jnp.concatenate([right_ref[...], left_ref[...]], axis=0)
    bias = jnp.concatenate([right_bias_ref[...], left_bias_ref[...]], axis=1)
    bias = jnp.broadcast_to(bias, (128, 64)).T
    copies[0].wait()
    x = x_ref[...].astype(F32).reshape(512, 256)
    centre = jnp.mean(x, axis=-1, keepdims=True)
    shifted = x - centre
    spread = jnp.mean(shifted * shifted, axis=-1, keepdims=True)
    normed = shifted * lax.rsqrt(spread + 1e-05) * gain_ref[...] + offset_ref[...]
    rows = lax.dot_general(both, normed.astype(BF16), NT, preferred_element_type=F32)
    rows = (rows + jnp.concatenate([bias] * 4, axis=1)).astype(BF16)
    rows = jnp.dot(rows, move, preferred_element_type=F32).astype(BF16)
    for r in range(4):
        for to in range(32):
            right_out[to, r * 32 : r * 32 + 32, :] = rows[:32, r * 128 : r * 128 + 128]
        left_out[r * 32 : r * 32 + 32, :] = rows[32:, r * 128 : r * 128 + 128]
    for copy in copies[7:]:
        copy.wait()
    map_out[:1024, :] = map_ref[...].astype(F32)
    map_out[1024:, :] = jnp.broadcast_to(bias_ref[...], (8, 128))


def join_kernel(own_ref, other_ref, out_ref):
    here = lax.axis_index("zu")
    out_ref[here] = own_ref[...]
    out_ref[1 - here] = other_ref[...]


def select_kernel(got_ref, out_ref):
    core = lax.axis_index("core")
    for zu in range(2):
        for block in range(2):
            for half in range(2):
                row = pl.multiple_of((half * 2 + core) * 32, 32)
                out_ref[zu, block, half * 32 : half * 32 + 32, :] = got_ref[block, zu, pl.ds(row, 32), :]


def pair_kernel(left_ref, right_ref, map_ref, out_ref, bias_out, a32, a16, x16, wide_ref, res):
    bias_out[...] = map_ref[1024:1025, :]
    for t in range(8):
        zl = t % 2 * 4 + t // 2 % 2 * 2 + t // 4
        for block in range(2):
            for half in range(2):
                a32[pl.ds(block * 512 + zl * 2 + half, 32, stride=16), :] = left_ref[
                    t, block, half * 32 : half * 32 + 32, :
                ].astype(F32)
    for block in range(2):
        a16[:, block * 128 : block * 128 + 128] = a32[block * 512 : block * 512 + 512, :].astype(BF16)
    wide_ref[...] = jnp.zeros_like(wide_ref)
    for c in range(32):
        for r in range(4):
            wide_ref[c * 128 + r * 32 : c * 128 + r * 32 + 32, r * 128 : r * 128 + 128] = map_ref[
                c * 32 : c * 32 + 32, :
            ].astype(BF16)
    for first in range(0, 16, 4):
        chips = range(first, first + 4)
        right = [jnp.concatenate([right_ref[yx % 4 * 8 + k * 4 + yx // 4] for k in range(2)], axis=1) for yx in chips]
        right = jnp.concatenate(right, axis=0)
        outer = lax.dot_general(a16[...], right, NT, preferred_element_type=F32).astype(BF16)
        for k, yx in enumerate(chips):
            for c in range(32):
                x16[yx * 16 : yx * 16 + 16, c * 128 : c * 128 + 128] = outer[
                    c * 16 : c * 16 + 16, k * 128 : k * 128 + 128
                ]
    total = jnp.dot(x16[...], wide_ref[...], preferred_element_type=F32) * (1.0 / 512)
    for r in range(4):
        res[r * 256 : r * 256 + 256, :] = total[:, r * 128 : r * 128 + 128]
    for k in range(8):
        for half in range(2):
            to = half * 8 + k
            for r in range(4):
                rows = res[pl.ds(r * 256 + k * 2 + half, 16, stride=16), :]
                out_ref[to, :, r * 128 : r * 128 + 128] = rows.astype(BF16)


def final_kernel(parts_ref, bias_ref, out_ref, rows):
    for zl in range(8):
        summed = parts_ref[zl].astype(F32) + parts_ref[8 + zl].astype(F32)
        for r in range(4):
            rows[pl.ds(zl * 4 + r, 16, stride=32), :] = summed[:, r * 128 : r * 128 + 128] + bias_ref[...]
    out_ref[...] = rows[...].astype(BF16)


def params(mib):
    return pltpu.CompilerParams(vmem_limit_bytes=mib * 2**20)


def shape(*dims, dtype=BF16):
    return jax.ShapeDtypeStruct(dims, dtype)


def local(x, gain, offset, first, first_bias, second, second_bias, mapping, final_bias):
    operands = (
        x,
        gain.reshape(1, 256),
        offset.reshape(1, 256),
        first.T,
        first_bias.reshape(1, 32),
        second.T,
        second_bias.reshape(1, 32),
    )
    operands += (mapping, final_bias.reshape(1, 128))
    operands = tuple(pltpu.with_memory_space_constraint(a, pltpu.HBM) for a in operands)
    right, left, mapping = pl.pallas_call(
        projection_kernel,
        out_shape=(shape(32, 128, 128), shape(128, 128), shape(1032, 128, dtype=F32)),
        in_specs=[pl.BlockSpec(memory_space=pltpu.HBM)] * 9,
        scratch_shapes=[pltpu.VMEM(a.shape, a.dtype) for a in operands] + [pltpu.SemaphoreType.DMA((9,))],
        compiler_params=params(16),
        name="projections",
    )(*operands)
    right = lax.all_to_all(right, ("x", "core", "y"), 0, 0)
    other = lax.ppermute(left, "zu", SWAP)
    left = pl.pallas_call(
        join_kernel,
        out_shape=shape(2, 128, 128),
        compiler_params=params(16),
        cost_estimate=pl.CostEstimate(flops=10**10, bytes_accessed=0, transcendentals=0),
        name="join",
    )(left, other)
    left = lax.all_gather(left, "core", axis=0)
    left = pl.pallas_call(
        select_kernel,
        out_shape=shape(2, 2, 64, 128),
        compiler_params=params(16),
        name="select",
    )(left)
    for axis in ("zv", "zp"):
        left = lax.all_gather(left, axis, axis=0)
    left = left.reshape(8, 2, 64, 128)

    parts, bias = pl.pallas_call(
        pair_kernel,
        out_shape=(shape(16, 16, 512), shape(1, 128, dtype=F32)),
        scratch_shapes=[
            pltpu.VMEM((1024, 128), F32),
            pltpu.VMEM((512, 256), BF16),
            pltpu.VMEM((256, 4096), BF16),
            pltpu.VMEM((4096, 512), BF16),
            pltpu.VMEM((1024, 128), F32),
        ],
        compiler_params=params(20),
        name="pair_block",
    )(left, right, mapping)
    parts = lax.all_to_all(parts, ("zh", "zu", "zv", "zp"), 0, 0)
    out = pl.pallas_call(
        final_kernel,
        out_shape=shape(512, 128),
        scratch_shapes=[pltpu.VMEM((512, 128), F32)],
        compiler_params=params(16),
        name="sum_and_bias",
    )(parts, bias)
    return out.reshape(1, 512, 128)


def solution(mesh):
    fine = Mesh(mesh.devices.reshape(4, 4, 2, 2, 2, 2, 2), AXES)
    placed = (P(("zh", "core"), ("y", "x", "zu", "zv", "zp"), None),) + (P(),) * 8
    return jax.shard_map(
        local, mesh=fine, in_specs=placed, out_specs=P(AXES, None, None), check_vma=False
    )
```

```python
import jax
import jax.numpy as jnp
from jax import lax
from jax.experimental import pallas as pl
from jax.experimental.pallas import tpu as pltpu
from jax.sharding import Mesh, PartitionSpec as P

F32 = jnp.float32
BF16 = jnp.bfloat16
AXES = ("y", "x", "zu", "zv", "zp", "zh", "core")
RING = ("zp", "zh", "zv", "zu")
SWAP = [(0, 1), (1, 0)]
NT = (((1,), (1,)), ((), ()))


def projection_kernel(
    x_hbm, gain_hbm, offset_hbm, left_hbm, left_bias_hbm, right_hbm, right_bias_hbm, map_hbm, bias_hbm,
    right_out, left_out, map_out, bias_out,
    x_ref, gain_ref, offset_ref, left_ref, left_bias_ref, right_ref, right_bias_ref, sems,
):
    sources = (x_hbm, gain_hbm, offset_hbm, left_hbm, left_bias_hbm, right_hbm, right_bias_hbm, map_hbm, bias_hbm)
    targets = (x_ref, gain_ref, offset_ref, left_ref, left_bias_ref, right_ref, right_bias_ref, map_out, bias_out)
    copies = [
        pltpu.make_async_copy(src, dst, sems.at[k]) for k, (src, dst) in enumerate(zip(sources, targets))
    ]
    for copy in copies:
        copy.start()
    source = lax.broadcasted_iota(jnp.int32, (512, 512), 0)
    target = lax.broadcasted_iota(jnp.int32, (512, 512), 1)
    move = (source == target % 128 * 4 + target // 128).astype(F32).astype(BF16)
    for copy in copies[1:7]:
        copy.wait()
    both = jnp.concatenate([right_ref[...], left_ref[...]], axis=0)
    bias = jnp.concatenate([right_bias_ref[...], left_bias_ref[...]], axis=1)
    bias = jnp.broadcast_to(bias, (128, 64)).T
    copies[0].wait()
    x = x_ref[...].astype(F32).reshape(512, 256)
    centre = jnp.mean(x, axis=-1, keepdims=True)
    shifted = x - centre
    spread = jnp.mean(shifted * shifted, axis=-1, keepdims=True)
    normed = shifted * lax.rsqrt(spread + 1e-05) * gain_ref[...] + offset_ref[...]
    rows = lax.dot_general(both, normed.astype(BF16), NT, preferred_element_type=F32)
    rows = (rows + jnp.concatenate([bias] * 4, axis=1)).astype(BF16)
    rows = jnp.dot(rows, move, preferred_element_type=F32).astype(BF16)
    for r in range(4):
        for to in range(32):
            right_out[to, r * 32 : r * 32 + 32, :] = rows[:32, r * 128 : r * 128 + 128]
        left_out[r * 32 : r * 32 + 32, :] = rows[32:, r * 128 : r * 128 + 128]
    for copy in copies[7:]:
        copy.wait()


def join_kernel(own_ref, other_ref, out_ref):
    here = lax.axis_index("zu")
    out_ref[here] = own_ref[...]
    out_ref[1 - here] = other_ref[...]


def select_kernel(got_ref, out_ref):
    core = lax.axis_index("core")
    for zu in range(2):
        for block in range(2):
            for half in range(2):
                row = pl.multiple_of((half * 2 + core) * 32, 32)
                out_ref[zu, block, half * 32 : half * 32 + 32, :] = got_ref[block, zu, pl.ds(row, 32), :]


def pair_kernel(left_ref, right_ref, map_ref, out_ref, a32, a16, x16, wide_ref, res):
    for t in range(8):
        zl = t % 2 * 4 + t // 2 % 2 * 2 + t // 4
        for block in range(2):
            for half in range(2):
                a32[pl.ds(block * 512 + zl * 2 + half, 32, stride=16), :] = left_ref[
                    t, block, half * 32 : half * 32 + 32, :
                ].astype(F32)
    for block in range(2):
        a16[:, block * 128 : block * 128 + 128] = a32[block * 512 : block * 512 + 512, :].astype(BF16)
    wide_ref[...] = jnp.zeros_like(wide_ref)
    for c in range(32):
        for r in range(4):
            wide_ref[c * 128 + r * 32 : c * 128 + r * 32 + 32, r * 128 : r * 128 + 128] = map_ref[
                c * 32 : c * 32 + 32, :
            ]
    for first in range(0, 16, 4):
        chips = range(first, first + 4)
        right = [jnp.concatenate([right_ref[yx % 4 * 8 + k * 4 + yx // 4] for k in range(2)], axis=1) for yx in chips]
        right = jnp.concatenate(right, axis=0)
        outer = lax.dot_general(a16[...], right, NT, preferred_element_type=F32).astype(BF16)
        for k, yx in enumerate(chips):
            for c in range(32):
                x16[yx * 16 : yx * 16 + 16, c * 128 : c * 128 + 128] = outer[
                    c * 16 : c * 16 + 16, k * 128 : k * 128 + 128
                ]
    total = jnp.dot(x16[...], wide_ref[...], preferred_element_type=F32) * (1.0 / 512)
    for r in range(4):
        res[r * 256 : r * 256 + 256, :] = total[:, r * 128 : r * 128 + 128]
    for k in range(8):
        for half in range(2):
            to = ring_rank(k, half)
            for r in range(4):
                rows = res[pl.ds(r * 256 + k * 2 + half, 16, stride=16), :]
                out_ref[to, :, r * 128 : r * 128 + 128] = rows.astype(BF16)


def ring_rank(zl, half):
    return zl % 2 * 8 + half * 4 + zl // 2 % 2 * 2 + zl // 4


def final_kernel(parts_ref, bias_ref, out_ref, rows):
    for zl in range(8):
        summed = parts_ref[ring_rank(zl, 0)].astype(F32) + parts_ref[ring_rank(zl, 1)].astype(F32)
        for r in range(4):
            rows[pl.ds(zl * 4 + r, 16, stride=32), :] = summed[:, r * 128 : r * 128 + 128] + bias_ref[...]
    out_ref[...] = rows[...].astype(BF16)


def params(mib):
    return pltpu.CompilerParams(vmem_limit_bytes=mib * 2**20)


def shape(*dims, dtype=BF16):
    return jax.ShapeDtypeStruct(dims, dtype)


def local(x, gain, offset, first, first_bias, second, second_bias, mapping, final_bias):
    operands = (
        x,
        gain.reshape(1, 256),
        offset.reshape(1, 256),
        first.T,
        first_bias.reshape(1, 32),
        second.T,
        second_bias.reshape(1, 32),
    )
    operands += (mapping, final_bias.reshape(1, 128))
    operands = tuple(pltpu.with_memory_space_constraint(a, pltpu.HBM) for a in operands)
    right, left, mapping, bias = pl.pallas_call(
        projection_kernel,
        out_shape=(shape(32, 128, 128), shape(128, 128), shape(1024, 128), shape(1, 128, dtype=F32)),
        in_specs=[pl.BlockSpec(memory_space=pltpu.HBM)] * 9,
        scratch_shapes=[pltpu.VMEM(a.shape, a.dtype) for a in operands[:7]] + [pltpu.SemaphoreType.DMA((9,))],
        compiler_params=params(16),
        name="projections",
    )(*operands)
    right = lax.all_to_all(right, ("x", "core", "y"), 0, 0)
    other = lax.ppermute(left, "zu", SWAP)
    left = pl.pallas_call(
        join_kernel,
        out_shape=shape(2, 128, 128),
        compiler_params=params(16),
        cost_estimate=pl.CostEstimate(flops=10**10, bytes_accessed=0, transcendentals=0),
        name="join",
    )(left, other)
    left = lax.all_gather(left, "core", axis=0)
    left = pl.pallas_call(
        select_kernel,
        out_shape=shape(2, 2, 64, 128),
        compiler_params=params(16),
        name="select",
    )(left)
    for axis in ("zv", "zp"):
        left = lax.all_gather(left, axis, axis=0)
    left = left.reshape(8, 2, 64, 128)

    parts = pl.pallas_call(
        pair_kernel,
        out_shape=shape(16, 16, 512),
        scratch_shapes=[
            pltpu.VMEM((1024, 128), F32),
            pltpu.VMEM((512, 256), BF16),
            pltpu.VMEM((256, 4096), BF16),
            pltpu.VMEM((4096, 512), BF16),
            pltpu.VMEM((1024, 128), F32),
        ],
        compiler_params=params(20),
        name="pair_block",
    )(left, right, mapping)
    parts = lax.all_to_all(parts, RING, 0, 0)
    out = pl.pallas_call(
        final_kernel,
        out_shape=shape(512, 128),
        scratch_shapes=[pltpu.VMEM((512, 128), F32)],
        compiler_params=params(16),
        name="sum_and_bias",
    )(parts, bias)
    return out.reshape(1, 512, 128)


def solution(mesh):
    fine = Mesh(mesh.devices.reshape(4, 4, 2, 2, 2, 2, 2), AXES)
    placed = (P(("zh", "core"), ("y", "x", "zu", "zv", "zp"), None),) + (P(),) * 8
    return jax.shard_map(
        local, mesh=fine, in_specs=placed, out_specs=P(AXES, None, None), check_vma=False
    )
```

```python
import jax
import jax.numpy as jnp
from jax import lax
from jax.experimental import pallas as pl
from jax.experimental.pallas import tpu as pltpu
from jax.sharding import Mesh, PartitionSpec as P

F32 = jnp.float32
BF16 = jnp.bfloat16
AXES = ("y", "x", "zu", "zv", "zp", "zh", "core")
RING = ("zp", "zh", "zv", "zu")
SWAP = [(0, 1), (1, 0)]
NT = (((1,), (1,)), ((), ()))


def projection_kernel(
    x_hbm, gain_hbm, offset_hbm, left_hbm, left_bias_hbm, right_hbm, right_bias_hbm, map_hbm, bias_hbm,
    right_out, left_out, map_out, bias_out,
    x_ref, gain_ref, offset_ref, left_ref, left_bias_ref, right_ref, right_bias_ref, sems,
):
    sources = (x_hbm, gain_hbm, offset_hbm, left_hbm, left_bias_hbm, right_hbm, right_bias_hbm, map_hbm, bias_hbm)
    targets = (x_ref, gain_ref, offset_ref, left_ref, left_bias_ref, right_ref, right_bias_ref, map_out, bias_out)
    copies = [
        pltpu.make_async_copy(src, dst, sems.at[k]) for k, (src, dst) in enumerate(zip(sources, targets))
    ]
    for copy in copies:
        copy.start()
    source = lax.broadcasted_iota(jnp.int32, (512, 512), 0)
    target = lax.broadcasted_iota(jnp.int32, (512, 512), 1)
    move = (source == target % 128 * 4 + target // 128).astype(F32).astype(BF16)
    for copy in copies[1:7]:
        copy.wait()
    both = jnp.concatenate([right_ref[...], left_ref[...]], axis=0)
    bias = jnp.concatenate([right_bias_ref[...], left_bias_ref[...]], axis=1)
    bias = jnp.broadcast_to(bias, (128, 64)).T
    copies[0].wait()
    x = x_ref[...].astype(F32).reshape(512, 256)
    centre = jnp.mean(x, axis=-1, keepdims=True)
    shifted = x - centre
    spread = jnp.mean(shifted * shifted, axis=-1, keepdims=True)
    normed = shifted * lax.rsqrt(spread + 1e-05) * gain_ref[...] + offset_ref[...]
    rows = lax.dot_general(both, normed.astype(BF16), NT, preferred_element_type=F32)
    rows = (rows + jnp.concatenate([bias] * 4, axis=1)).astype(BF16)
    rows = jnp.dot(rows, move, preferred_element_type=F32).astype(BF16)
    for r in range(4):
        for to in range(32):
            right_out[to, r * 32 : r * 32 + 32, :] = rows[:32, r * 128 : r * 128 + 128]
        left_out[r * 32 : r * 32 + 32, :] = rows[32:, r * 128 : r * 128 + 128]
    for copy in copies[7:]:
        copy.wait()


def join_kernel(own_ref, other_ref, out_ref):
    here = lax.axis_index("zu")
    out_ref[here] = own_ref[...]
    out_ref[1 - here] = other_ref[...]


def select_kernel(got_ref, out_ref):
    core = lax.axis_index("core")
    for zu in range(2):
        for block in range(2):
            for half in range(2):
                row = pl.multiple_of((half * 2 + core) * 32, 32)
                out_ref[zu, block, half * 32 : half * 32 + 32, :] = got_ref[block, zu, pl.ds(row, 32), :]


def pair_kernel(left_ref, right_ref, map_ref, out_ref, a32, a16, x16, wide_ref, res):
    for t in range(8):
        zl = t % 2 * 4 + t // 2 % 2 * 2 + t // 4
        for block in range(2):
            for half in range(2):
                a32[pl.ds(block * 512 + zl * 2 + half, 32, stride=16), :] = left_ref[
                    t, block, half * 32 : half * 32 + 32, :
                ].astype(F32)
    for block in range(2):
        a16[:, block * 128 : block * 128 + 128] = a32[block * 512 : block * 512 + 512, :].astype(BF16)
    wide_ref[...] = jnp.zeros_like(wide_ref)
    for c in range(32):
        for r in range(4):
            wide_ref[c * 128 + r * 32 : c * 128 + r * 32 + 32, r * 128 : r * 128 + 128] = map_ref[
                c * 32 : c * 32 + 32, :
            ]
    for first in range(0, 16, 4):
        chips = range(first, first + 4)
        right = [jnp.concatenate([right_ref[yx % 4 * 8 + k * 4 + yx // 4] for k in range(2)], axis=1) for yx in chips]
        right = jnp.concatenate(right, axis=0)
        outer = lax.dot_general(a16[...], right, NT, preferred_element_type=F32).astype(BF16)
        for k, yx in enumerate(chips):
            for c in range(32):
                x16[yx * 16 : yx * 16 + 16, c * 128 : c * 128 + 128] = outer[
                    c * 16 : c * 16 + 16, k * 128 : k * 128 + 128
                ]
    total = jnp.dot(x16[...], wide_ref[...], preferred_element_type=F32) * (1.0 / 512)
    for r in range(4):
        res[r * 256 : r * 256 + 256, :] = total[:, r * 128 : r * 128 + 128]
    for k in range(8):
        for half in range(2):
            to = ring_rank(k, half)
            for r in range(4):
                rows = res[pl.ds(r * 256 + k * 2 + half, 16, stride=16), :]
                out_ref[to, :, r * 128 : r * 128 + 128] = rows.astype(BF16)


def ring_rank(zl, half):
    return zl % 2 * 8 + half * 4 + zl // 2 % 2 * 2 + zl // 4


def final_kernel(parts_ref, bias_ref, out_ref, rows):
    for zl in range(8):
        summed = parts_ref[ring_rank(zl, 0)].astype(F32) + parts_ref[ring_rank(zl, 1)].astype(F32)
        for r in range(4):
            rows[pl.ds(zl * 4 + r, 16, stride=32), :] = summed[:, r * 128 : r * 128 + 128] + bias_ref[...]
    out_ref[...] = rows[...].astype(BF16)


def params(mib):
    return pltpu.CompilerParams(vmem_limit_bytes=mib * 2**20)


def shape(*dims, dtype=BF16):
    return jax.ShapeDtypeStruct(dims, dtype)


def local(x, gain, offset, first, first_bias, second, second_bias, mapping, final_bias):
    operands = (
        x,
        gain.reshape(1, 256),
        offset.reshape(1, 256),
        first.T,
        first_bias.reshape(1, 32),
        second.T,
        second_bias.reshape(1, 32),
        mapping,
        final_bias.reshape(1, 128),
    )
    operands = tuple(pltpu.with_memory_space_constraint(a, pltpu.HBM) for a in operands)
    right, left, mapping, bias = pl.pallas_call(
        projection_kernel,
        out_shape=(shape(32, 128, 128), shape(128, 128), shape(1024, 128), shape(1, 128, dtype=F32)),
        in_specs=[pl.BlockSpec(memory_space=pltpu.HBM)] * 9,
        scratch_shapes=[pltpu.VMEM(a.shape, a.dtype) for a in operands[:7]] + [pltpu.SemaphoreType.DMA((9,))],
        compiler_params=params(16),
        name="projections",
    )(*operands)
    right = lax.all_to_all(right, ("x", "core", "y"), 0, 0)
    other = lax.ppermute(left, "zu", SWAP)
    left = pl.pallas_call(
        join_kernel,
        out_shape=shape(2, 128, 128),
        compiler_params=params(16),
        cost_estimate=pl.CostEstimate(flops=10**10, bytes_accessed=0, transcendentals=0),
        name="join",
    )(left, other)
    left = lax.all_gather(left, "core", axis=0)
    left = pl.pallas_call(
        select_kernel,
        out_shape=shape(2, 2, 64, 128),
        compiler_params=params(16),
        name="select",
    )(left)
    for axis in ("zv", "zp"):
        left = lax.all_gather(left, axis, axis=0)
    left = left.reshape(8, 2, 64, 128)

    parts = pl.pallas_call(
        pair_kernel,
        out_shape=shape(16, 16, 512),
        scratch_shapes=[
            pltpu.VMEM((1024, 128), F32),
            pltpu.VMEM((512, 256), BF16),
            pltpu.VMEM((256, 4096), BF16),
            pltpu.VMEM((4096, 512), BF16),
            pltpu.VMEM((1024, 128), F32),
        ],
        compiler_params=params(20),
        name="pair_block",
    )(left, right, mapping)
    parts = lax.all_to_all(parts, RING, 0, 0)
    out = pl.pallas_call(
        final_kernel,
        out_shape=shape(512, 128),
        scratch_shapes=[pltpu.VMEM((512, 128), F32)],
        compiler_params=params(16),
        name="sum_and_bias",
    )(parts, bias)
    return out.reshape(1, 512, 128)


def solution(mesh):
    fine = Mesh(mesh.devices.reshape(4, 4, 2, 2, 2, 2, 2), AXES)
    placed = (P(("zh", "core"), ("y", "x", "zu", "zv", "zp"), None),) + (P(),) * 8
    return jax.shard_map(
        local, mesh=fine, in_specs=placed, out_specs=P(AXES, None, None), check_vma=False
    )
```

```python
import jax
import jax.numpy as jnp
from jax import lax
from jax.experimental import pallas as pl
from jax.experimental.pallas import tpu as pltpu
from jax.sharding import Mesh, PartitionSpec as P

F32 = jnp.float32
BF16 = jnp.bfloat16
AXES = ("y", "x", "zu", "zv", "zp", "zh", "core")
RING = ("zp", "zh", "zv", "zu")
SWAP = [(0, 1), (1, 0)]
NT = (((1,), (1,)), ((), ()))


def projection_kernel(
    x_hbm, gain_hbm, offset_hbm, left_hbm, left_bias_hbm, right_hbm, right_bias_hbm, map_hbm, bias_hbm,
    right_out, left_out, map_out, bias_out,
    x_ref, gain_ref, offset_ref, left_ref, left_bias_ref, right_ref, right_bias_ref, sems,
):
    sources = (x_hbm, gain_hbm, offset_hbm, left_hbm, left_bias_hbm, right_hbm, right_bias_hbm, map_hbm, bias_hbm)
    targets = (x_ref, gain_ref, offset_ref, left_ref, left_bias_ref, right_ref, right_bias_ref, map_out, bias_out)
    copies = [
        pltpu.make_async_copy(src, dst, sems.at[k]) for k, (src, dst) in enumerate(zip(sources, targets))
    ]
    for copy in copies:
        copy.start()
    source = lax.broadcasted_iota(jnp.int32, (512, 512), 0)
    target = lax.broadcasted_iota(jnp.int32, (512, 512), 1)
    move = (source == target % 128 * 4 + target // 128).astype(F32).astype(BF16)
    for copy in copies[1:7]:
        copy.wait()
    both = jnp.concatenate([right_ref[...], left_ref[...]], axis=0)
    bias = jnp.concatenate([right_bias_ref[...], left_bias_ref[...]], axis=1)
    bias = jnp.broadcast_to(bias, (128, 64)).T
    copies[0].wait()
    x = x_ref[...].astype(F32).reshape(512, 256)
    centre = jnp.mean(x, axis=-1, keepdims=True)
    shifted = x - centre
    spread = jnp.mean(shifted * shifted, axis=-1, keepdims=True)
    normed = shifted * lax.rsqrt(spread + 1e-05) * gain_ref[...] + offset_ref[...]
    rows = lax.dot_general(both, normed.astype(BF16), NT, preferred_element_type=F32)
    rows = (rows + jnp.concatenate([bias] * 4, axis=1)).astype(BF16)
    rows = jnp.dot(rows, move, preferred_element_type=F32).astype(BF16)
    for r in range(4):
        for to in range(32):
            right_out[to, r * 32 : r * 32 + 32, :] = rows[:32, r * 128 : r * 128 + 128]
        left_out[r * 32 : r * 32 + 32, :] = rows[32:, r * 128 : r * 128 + 128]
    for copy in copies[7:]:
        copy.wait()


def join_kernel(own_ref, other_ref, out_ref):
    here = lax.axis_index("zu")
    out_ref[here] = own_ref[...]
    out_ref[1 - here] = other_ref[...]


def select_kernel(got_ref, out_ref):
    core = lax.axis_index("core")
    for zu in range(2):
        for block in range(2):
            for half in range(2):
                row = pl.multiple_of((half * 2 + core) * 32, 32)
                out_ref[zu, block, half * 32 : half * 32 + 32, :] = got_ref[block, zu, pl.ds(row, 32), :]


def prepare_kernel(left_ref, a16, a32):
    for t in range(8):
        zl = t % 2 * 4 + t // 2 % 2 * 2 + t // 4
        for block in range(2):
            for half in range(2):
                a32[pl.ds(block * 512 + zl * 2 + half, 32, stride=16), :] = left_ref[
                    t, block, half * 32 : half * 32 + 32, :
                ].astype(F32)
    for block in range(2):
        a16[:, block * 128 : block * 128 + 128] = a32[block * 512 : block * 512 + 512, :].astype(BF16)


def pair_kernel(a16, right_ref, map_ref, out_ref, x16, wide_ref, res):
    wide_ref[...] = jnp.zeros_like(wide_ref)
    for c in range(32):
        for r in range(4):
            wide_ref[c * 128 + r * 32 : c * 128 + r * 32 + 32, r * 128 : r * 128 + 128] = map_ref[
                c * 32 : c * 32 + 32, :
            ]
    for first in range(0, 16, 4):
        chips = range(first, first + 4)
        right = [jnp.concatenate([right_ref[yx % 4 * 8 + k * 4 + yx // 4] for k in range(2)], axis=1) for yx in chips]
        right = jnp.concatenate(right, axis=0)
        outer = lax.dot_general(a16[...], right, NT, preferred_element_type=F32).astype(BF16)
        for k, yx in enumerate(chips):
            for c in range(32):
                x16[yx * 16 : yx * 16 + 16, c * 128 : c * 128 + 128] = outer[
                    c * 16 : c * 16 + 16, k * 128 : k * 128 + 128
                ]
    total = jnp.dot(x16[...], wide_ref[...], preferred_element_type=F32) * (1.0 / 512)
    for r in range(4):
        res[r * 256 : r * 256 + 256, :] = total[:, r * 128 : r * 128 + 128]
    for k in range(8):
        for half in range(2):
            to = ring_rank(k, half)
            for r in range(4):
                rows = res[pl.ds(r * 256 + k * 2 + half, 16, stride=16), :]
                out_ref[to, :, r * 128 : r * 128 + 128] = rows.astype(BF16)


def ring_rank(zl, half):
    return zl % 2 * 8 + half * 4 + zl // 2 % 2 * 2 + zl // 4


def final_kernel(parts_ref, bias_ref, out_ref, rows):
    for zl in range(8):
        summed = parts_ref[ring_rank(zl, 0)].astype(F32) + parts_ref[ring_rank(zl, 1)].astype(F32)
        for r in range(4):
            rows[pl.ds(zl * 4 + r, 16, stride=32), :] = summed[:, r * 128 : r * 128 + 128] + bias_ref[...]
    out_ref[...] = rows[...].astype(BF16)


def params(mib):
    return pltpu.CompilerParams(vmem_limit_bytes=mib * 2**20)


def shape(*dims, dtype=BF16):
    return jax.ShapeDtypeStruct(dims, dtype)


def local(x, gain, offset, first, first_bias, second, second_bias, mapping, final_bias):
    operands = (
        x,
        gain.reshape(1, 256),
        offset.reshape(1, 256),
        first.T,
        first_bias.reshape(1, 32),
        second.T,
        second_bias.reshape(1, 32),
    )
    operands += (mapping, final_bias.reshape(1, 128))
    operands = tuple(pltpu.with_memory_space_constraint(a, pltpu.HBM) for a in operands)
    right, left, mapping, bias = pl.pallas_call(
        projection_kernel,
        out_shape=(shape(32, 128, 128), shape(128, 128), shape(1024, 128), shape(1, 128, dtype=F32)),
        in_specs=[pl.BlockSpec(memory_space=pltpu.HBM)] * 9,
        scratch_shapes=[pltpu.VMEM(a.shape, a.dtype) for a in operands[:7]] + [pltpu.SemaphoreType.DMA((9,))],
        compiler_params=params(16),
        name="projections",
    )(*operands)
    right = lax.all_to_all(right, ("x", "core", "y"), 0, 0)
    other = lax.ppermute(left, "zu", SWAP)
    left = pl.pallas_call(
        join_kernel,
        out_shape=shape(2, 128, 128),
        compiler_params=params(16),
        cost_estimate=pl.CostEstimate(flops=10**10, bytes_accessed=0, transcendentals=0),
        name="join",
    )(left, other)
    left = lax.all_gather(left, "core", axis=0)
    left = pl.pallas_call(
        select_kernel,
        out_shape=shape(2, 2, 64, 128),
        compiler_params=params(16),
        name="select",
    )(left)
    for axis in ("zv", "zp"):
        left = lax.all_gather(left, axis, axis=0)
    left = left.reshape(8, 2, 64, 128)

    left = pl.pallas_call(
        prepare_kernel,
        out_shape=shape(512, 256),
        scratch_shapes=[pltpu.VMEM((1024, 128), F32)],
        compiler_params=params(12),
        name="prepare",
    )(left)
    parts = pl.pallas_call(
        pair_kernel,
        out_shape=shape(16, 16, 512),
        scratch_shapes=[
            pltpu.VMEM((256, 4096), BF16),
            pltpu.VMEM((4096, 512), BF16),
            pltpu.VMEM((1024, 128), F32),
        ],
        compiler_params=params(20),
        name="pair_block",
    )(left, right, mapping)
    parts = lax.all_to_all(parts, RING, 0, 0)
    out = pl.pallas_call(
        final_kernel,
        out_shape=shape(512, 128),
        scratch_shapes=[pltpu.VMEM((512, 128), F32)],
        compiler_params=params(16),
        name="sum_and_bias",
    )(parts, bias)
    return out.reshape(1, 512, 128)


def solution(mesh):
    fine = Mesh(mesh.devices.reshape(4, 4, 2, 2, 2, 2, 2), AXES)
    placed = (P(("zh", "core"), ("y", "x", "zu", "zv", "zp"), None),) + (P(),) * 8
    return jax.shard_map(
        local, mesh=fine, in_specs=placed, out_specs=P(AXES, None, None), check_vma=False
    )
```

```python
import jax
import jax.numpy as jnp
from jax import lax
from jax.experimental import pallas as pl
from jax.experimental.pallas import tpu as pltpu
from jax.sharding import Mesh, PartitionSpec as P

F32 = jnp.float32
BF16 = jnp.bfloat16
AXES = ("y", "x", "zu", "zv", "zp", "zh", "core")
RING = ("zp", "zh", "zv", "zu")
SWAP = [(0, 1), (1, 0)]
NT = (((1,), (1,)), ((), ()))


def projection_kernel(
    x_hbm, gain_hbm, offset_hbm, left_hbm, left_bias_hbm, right_hbm, right_bias_hbm, map_hbm, bias_hbm,
    right_out, left_out, map_out, bias_out,
    x_ref, gain_ref, offset_ref, left_ref, left_bias_ref, right_ref, right_bias_ref, sems,
):
    sources = (x_hbm, gain_hbm, offset_hbm, left_hbm, left_bias_hbm, right_hbm, right_bias_hbm, map_hbm, bias_hbm)
    targets = (x_ref, gain_ref, offset_ref, left_ref, left_bias_ref, right_ref, right_bias_ref, map_out, bias_out)
    copies = [
        pltpu.make_async_copy(src, dst, sems.at[k]) for k, (src, dst) in enumerate(zip(sources, targets))
    ]
    for copy in copies:
        copy.start()
    source = lax.broadcasted_iota(jnp.int32, (512, 512), 0)
    target = lax.broadcasted_iota(jnp.int32, (512, 512), 1)
    move = (source == target % 128 * 4 + target // 128).astype(F32).astype(BF16)
    for copy in copies[1:7]:
        copy.wait()
    both = jnp.concatenate([right_ref[...], left_ref[...]], axis=0)
    bias = jnp.concatenate([right_bias_ref[...], left_bias_ref[...]], axis=1)
    bias = jnp.broadcast_to(bias, (128, 64)).T
    copies[0].wait()
    x = x_ref[...].astype(F32).reshape(512, 256)
    centre = jnp.mean(x, axis=-1, keepdims=True)
    shifted = x - centre
    spread = jnp.mean(shifted * shifted, axis=-1, keepdims=True)
    normed = shifted * lax.rsqrt(spread + 1e-05) * gain_ref[...] + offset_ref[...]
    rows = lax.dot_general(both, normed.astype(BF16), NT, preferred_element_type=F32)
    rows = (rows + jnp.concatenate([bias] * 4, axis=1)).astype(BF16)
    rows = jnp.dot(rows, move, preferred_element_type=F32).astype(BF16)
    for r in range(4):
        for to in range(32):
            right_out[to, r * 32 : r * 32 + 32, :] = rows[:32, r * 128 : r * 128 + 128]
        left_out[r * 32 : r * 32 + 32, :] = rows[32:, r * 128 : r * 128 + 128]
    for copy in copies[7:]:
        copy.wait()


def join_kernel(own_ref, other_ref, out_ref):
    here = lax.axis_index("zu")
    out_ref[here] = own_ref[...]
    out_ref[1 - here] = other_ref[...]


def select_kernel(got_ref, out_ref):
    core = lax.axis_index("core")
    for zu in range(2):
        for block in range(2):
            for half in range(2):
                row = pl.multiple_of((half * 2 + core) * 32, 32)
                out_ref[zu, block, half * 32 : half * 32 + 32, :] = got_ref[block, zu, pl.ds(row, 32), :]


def prepare_kernel(left_ref, a16, a32):
    for t in range(8):
        zl = t % 2 * 4 + t // 2 % 2 * 2 + t // 4
        for block in range(2):
            for half in range(2):
                a32[pl.ds(block * 512 + zl * 2 + half, 32, stride=16), :] = left_ref[
                    t, block, half * 32 : half * 32 + 32, :
                ].astype(F32)
    for block in range(2):
        a16[:, block * 128 : block * 128 + 128] = a32[block * 512 : block * 512 + 512, :].astype(BF16)


def pair_kernel(a16, right_ref, map_ref, out_ref, x16, wide_ref, res):
    wide_ref[...] = jnp.zeros_like(wide_ref)
    for c in range(32):
        for r in range(4):
            wide_ref[c * 128 + r * 32 : c * 128 + r * 32 + 32, r * 128 : r * 128 + 128] = map_ref[
                c * 32 : c * 32 + 32, :
            ]
    for first in range(0, 16, 4):
        chips = range(first, first + 4)
        right = [jnp.concatenate([right_ref[yx % 4 * 8 + k * 4 + yx // 4] for k in range(2)], axis=1) for yx in chips]
        right = jnp.concatenate(right, axis=0)
        outer = lax.dot_general(a16[...], right, NT, preferred_element_type=F32).astype(BF16)
        for k, yx in enumerate(chips):
            for c in range(32):
                x16[yx * 16 : yx * 16 + 16, c * 128 : c * 128 + 128] = outer[
                    c * 16 : c * 16 + 16, k * 128 : k * 128 + 128
                ]
    for first in range(0, 4, 2):
        lanes = wide_ref[:, first * 128 : first * 128 + 256]
        total = jnp.dot(x16[...], lanes, preferred_element_type=F32) * (1.0 / 512)
        for r in range(first, first + 2):
            res[r * 256 : r * 256 + 256, :] = total[:, (r - first) * 128 : (r - first) * 128 + 128]
            for k in range(8):
                for half in range(2):
                    rows = res[pl.ds(r * 256 + k * 2 + half, 16, stride=16), :]
                    out_ref[ring_rank(k, half), :, r * 128 : r * 128 + 128] = rows.astype(BF16)


def ring_rank(zl, half):
    return zl % 2 * 8 + half * 4 + zl // 2 % 2 * 2 + zl // 4


def final_kernel(parts_ref, bias_ref, out_ref, rows):
    for zl in range(8):
        summed = parts_ref[ring_rank(zl, 0)].astype(F32) + parts_ref[ring_rank(zl, 1)].astype(F32)
        for r in range(4):
            rows[pl.ds(zl * 4 + r, 16, stride=32), :] = summed[:, r * 128 : r * 128 + 128] + bias_ref[...]
    out_ref[...] = rows[...].astype(BF16)


def params(mib):
    return pltpu.CompilerParams(vmem_limit_bytes=mib * 2**20)


def shape(*dims, dtype=BF16):
    return jax.ShapeDtypeStruct(dims, dtype)


def local(x, gain, offset, first, first_bias, second, second_bias, mapping, final_bias):
    operands = (
        x,
        gain.reshape(1, 256),
        offset.reshape(1, 256),
        first.T,
        first_bias.reshape(1, 32),
        second.T,
        second_bias.reshape(1, 32),
    )
    operands += (mapping, final_bias.reshape(1, 128))
    operands = tuple(pltpu.with_memory_space_constraint(a, pltpu.HBM) for a in operands)
    right, left, mapping, bias = pl.pallas_call(
        projection_kernel,
        out_shape=(shape(32, 128, 128), shape(128, 128), shape(1024, 128), shape(1, 128, dtype=F32)),
        in_specs=[pl.BlockSpec(memory_space=pltpu.HBM)] * 9,
        scratch_shapes=[pltpu.VMEM(a.shape, a.dtype) for a in operands[:7]] + [pltpu.SemaphoreType.DMA((9,))],
        compiler_params=params(16),
        name="projections",
    )(*operands)
    right = lax.all_to_all(right, ("x", "core", "y"), 0, 0)
    other = lax.ppermute(left, "zu", SWAP)
    left = pl.pallas_call(
        join_kernel,
        out_shape=shape(2, 128, 128),
        compiler_params=params(16),
        cost_estimate=pl.CostEstimate(flops=10**10, bytes_accessed=0, transcendentals=0),
        name="join",
    )(left, other)
    left = lax.all_gather(left, "core", axis=0)
    left = pl.pallas_call(
        select_kernel,
        out_shape=shape(2, 2, 64, 128),
        compiler_params=params(16),
        name="select",
    )(left)
    for axis in ("zv", "zp"):
        left = lax.all_gather(left, axis, axis=0)
    left = left.reshape(8, 2, 64, 128)

    left = pl.pallas_call(
        prepare_kernel,
        out_shape=shape(512, 256),
        scratch_shapes=[pltpu.VMEM((1024, 128), F32)],
        compiler_params=params(12),
        name="prepare",
    )(left)
    parts = pl.pallas_call(
        pair_kernel,
        out_shape=shape(16, 16, 512),
        scratch_shapes=[
            pltpu.VMEM((256, 4096), BF16),
            pltpu.VMEM((4096, 512), BF16),
            pltpu.VMEM((1024, 128), F32),
        ],
        compiler_params=params(20),
        name="pair_block",
    )(left, right, mapping)
    parts = lax.all_to_all(parts, RING, 0, 0)
    out = pl.pallas_call(
        final_kernel,
        out_shape=shape(512, 128),
        scratch_shapes=[pltpu.VMEM((512, 128), F32)],
        compiler_params=params(16),
        name="sum_and_bias",
    )(parts, bias)
    return out.reshape(1, 512, 128)


def solution(mesh):
    fine = Mesh(mesh.devices.reshape(4, 4, 2, 2, 2, 2, 2), AXES)
    placed = (P(("zh", "core"), ("y", "x", "zu", "zv", "zp"), None),) + (P(),) * 8
    return jax.shard_map(
        local, mesh=fine, in_specs=placed, out_specs=P(AXES, None, None), check_vma=False
    )
```
